32 devices in a mesh: row: 16 (over z, y, x), col: 2 (over core).
Axes of the slice: x: 2, y: 2, z: 4, core: 2. Of those that a mesh axis runs over, the one named last changes fastest.
Arguments:
- matrix: float32 [1, 2048, 8, 256], P(None, 'row', None, 'col'), may hold values from -8 to 8, as said below
Outputs:
- reduced: float32 [1, 2048, 8, 256], P(None, 'row', None, 'col')
The draws below stay inside these ranges and needn't reach their ends.
Inputs may be any that keep to these rules, and one draw needn't show every extreme that they name: matrix holds a symmetric matrix.
All inputs are finite; a program needn't handle non-finite values.
Results may differ from the reference program's by a relative error of at most 0.0003.
Values sent between devices are 32-bit elements; how exact they have to be, the bound alone decides.
A program may use at most 64 MiB of HBM per device.

```python
import jax
import jax.numpy as jnp
from jax import lax

TILE = 128
TR_DEV = 1
TC_DEV = 8
ORDER = 2048


def draw_matrix(key, part):
    places = jnp.arange(ORDER, dtype=jnp.int32)
    near = (jnp.abs(places[:, None] - places[None, :]) < 2 * TILE).astype(jnp.float32)
    raw = jax.random.normal(key, (ORDER, ORDER), jnp.float32)
    sym = (raw + raw.T) * 0.70710678
    sym = sym * (1.0 + 3.0 * near)
    sym = jnp.clip(sym, -8.0, 8.0)
    return sym.reshape(TR_DEV, ORDER // TR_DEV, TC_DEV, ORDER // TC_DEV)


def setup_inputs(seed: int = 0) -> dict:
    seeds = jax.random.split(jax.random.key(seed), 2)
    matrix = draw_matrix(jax.random.fold_in(seeds[1], 71), 0)
    return {"matrix": matrix}


def reference(matrix):
    highest = lax.Precision.HIGHEST
    whole = matrix.reshape(ORDER, ORDER)
    panel = whole[TILE:, :TILE]
    gram = jnp.dot(panel.T.astype(jnp.float32), panel.astype(jnp.float32), precision=highest, preferred_element_type=jnp.float32)
    lower = jnp.linalg.cholesky(gram)
    basis = jax.scipy.linalg.solve_triangular(lower, panel.T, lower=True).T
    identity = jnp.eye(TILE, dtype=jnp.float32)
    top = basis[:TILE]
    coupling = jnp.linalg.solve(identity + top.T, identity)
    vectors = jnp.concatenate([jnp.zeros((TILE, TILE), jnp.float32), basis.at[:TILE].add(identity)], axis=0)
    image = jnp.dot(whole.astype(jnp.float32), vectors.astype(jnp.float32), precision=highest, preferred_element_type=jnp.float32)
    middle = jnp.dot(vectors.T.astype(jnp.float32), image.astype(jnp.float32), precision=highest, preferred_element_type=jnp.float32)
    sandwich = jnp.dot(coupling.T, jnp.dot(middle, coupling, precision=highest), precision=highest)
    update = jnp.dot(image, coupling, precision=highest) - 0.5 * jnp.dot(vectors, sandwich, precision=highest)

    def one_block(index):
        start = (index * TILE).astype(jnp.int32)
        rows = lax.dynamic_slice_in_dim(whole, start, TILE, 0)
        upd_rows = lax.dynamic_slice_in_dim(update, start, TILE, 0)
        vec_rows = lax.dynamic_slice_in_dim(vectors, start, TILE, 0)
        first = jnp.dot(upd_rows.astype(jnp.float32), vectors.T.astype(jnp.float32), precision=highest, preferred_element_type=jnp.float32)
        second = jnp.dot(vec_rows.astype(jnp.float32), update.T.astype(jnp.float32), precision=highest, preferred_element_type=jnp.float32)
        return rows - first - second
    blocks = lax.map(one_block, jnp.arange(ORDER // TILE, dtype=jnp.int32))
    return blocks.reshape(matrix.shape)
```

```python
import functools

import jax
import jax.numpy as jnp
from jax import lax
from jax.experimental import pallas as pl
from jax.experimental.pallas import tpu as pltpu
from jax.sharding import PartitionSpec as P

MESH = pl.DeviceIdType.MESH
VMEM_LIMIT = 48 * 1024 * 1024


def product(left, right, contract):
    return lax.dot_general(
        left,
        right,
        (contract, ((), ())),
        precision=lax.Precision.HIGHEST,
        preferred_element_type=jnp.float32,
    )


TN = ((0,), (0,))
NN = ((1,), (0,))
NT = ((1,), (1,))


def exchange_start(source, slots, send_sem, recv_sem, cols):
    c = lax.axis_index("col")
    r = lax.axis_index("row")
    copies = []
    for step in range(1, cols):
        copy = pltpu.make_async_remote_copy(
            src_ref=source,
            dst_ref=slots.at[step - 1],
            send_sem=send_sem.at[step - 1],
            recv_sem=recv_sem.at[step - 1],
            device_id=(r, lax.rem(c + step, cols)),
            device_id_type=MESH,
        )
        copy.start()
        copies.append(copy)
    return copies


def spread(source, dest, slot, rows, target_col, send_sem, recv_sem, wait):
    r = lax.axis_index("row")

    def body(step, carry):
        copy = pltpu.make_async_remote_copy(
            src_ref=source,
            dst_ref=dest.at[slot],
            send_sem=send_sem.at[step],
            recv_sem=recv_sem.at[slot],
            device_id=(lax.rem(r + step, rows), target_col),
            device_id_type=MESH,
        )
        if wait:
            copy.wait_send()
        else:
            copy.start()
        return carry

    lax.fori_loop(1, rows, body, 0)


def arrive(source, dest, slot, recv_sem):
    pltpu.make_async_remote_copy(
        src_ref=source,
        dst_ref=dest.at[slot],
        send_sem=recv_sem.at[slot],
        recv_sem=recv_sem.at[slot],
        device_id=(lax.axis_index("row"), lax.axis_index("col")),
        device_id_type=MESH,
    ).wait_recv()


def greet(rows, cols, root_col, sends):
    r = lax.axis_index("row")
    c = lax.axis_index("col")
    barrier = pltpu.get_barrier_semaphore()

    def body(slot, carry):
        root = slot * cols + c

        @pl.when(root != r)
        def _():
            pl.semaphore_signal(barrier, inc=1, device_id=(root, root_col), device_id_type=MESH)

        return carry

    lax.fori_loop(0, rows // cols, body, 0)
    for step in range(1, cols):
        pl.semaphore_signal(
            barrier, inc=1, device_id=(r, lax.rem(c + step, cols)), device_id_type=MESH
        )

    @pl.when(sends)
    def _():
        pl.semaphore_wait(barrier, rows - 1 + cols - 1)

    @pl.when(jnp.logical_not(sends))
    def _():
        pl.semaphore_wait(barrier, cols - 1)


def gather_kernel(
    rows, cols, local_ref, tiles_ref, own_ref, sums_ref,
    parts, slots, send_sem, recv_sem, own_send, own_recv, ex_send, ex_recv,
):
    r = lax.axis_index("row")
    c = lax.axis_index("col")
    is_root = c == 0
    count = rows // cols
    slot_own = r // cols
    own_col = lax.rem(r, cols)

    @pl.when(is_root)
    def _():
        own_ref[...] = local_ref[0, :, 0, :]

    greet(rows, cols, 0, is_root)

    @pl.when(is_root)
    def _():
        for peer in range(1, cols):
            pltpu.make_async_remote_copy(
                src_ref=own_ref, dst_ref=own_ref, send_sem=own_send.at[peer - 1],
                recv_sem=own_recv, device_id=(r, peer), device_id_type=MESH,
            ).start()
        spread(own_ref, tiles_ref, slot_own, rows, own_col, send_sem, recv_sem, False)

    @pl.when(jnp.logical_not(is_root))
    def _():
        pltpu.make_async_remote_copy(
            src_ref=own_ref, dst_ref=own_ref, send_sem=own_recv,
            recv_sem=own_recv, device_id=(r, c), device_id_type=MESH,
        ).wait_recv()

    @pl.when(own_col == c)
    def _():
        tiles_ref[slot_own] = own_ref[...]

    parts[...] = jnp.zeros_like(parts)

    def gram_step(slot, carry):
        tile = slot * cols + c

        @pl.when(tile != r)
        def _():
            arrive(own_ref, tiles_ref, slot, recv_sem)

        @pl.when(tile != 0)
        def _():
            block = tiles_ref[slot]
            parts[0] += product(block, block, TN)

        @pl.when(tile == 1)
        def _():
            parts[1] = tiles_ref[slot]

        return carry

    lax.fori_loop(0, count, gram_step, 0)
    copies = exchange_start(parts, slots, ex_send, ex_recv, cols)
    for copy in copies:
        copy.wait()
    total = parts[...]
    for step in range(cols - 1):
        total = total + slots[step]
    sums_ref[...] = total

    @pl.when(is_root)
    def _():
        for peer in range(1, cols):
            pltpu.make_async_remote_copy(
                src_ref=own_ref, dst_ref=own_ref, send_sem=own_send.at[peer - 1],
                recv_sem=own_recv, device_id=(r, peer), device_id_type=MESH,
            ).wait_send()
        spread(own_ref, tiles_ref, slot_own, rows, own_col, send_sem, recv_sem, True)


def image_kernel(
    rows, cols, local_ref, vec_ref, image_ref, own_ref, middle_ref,
    part, slots, mid, mid_slots, send_sem, recv_sem, ex_send, ex_recv, mid_send, mid_recv,
):
    r = lax.axis_index("row")
    c = lax.axis_index("col")
    count = rows // cols
    slot_own = r // cols
    sends = lax.rem(r, cols) == c
    total = product(local_ref[0, :, 0, :], vec_ref[0], NN)
    for slot in range(1, count):
        total = total + product(local_ref[0, :, slot, :], vec_ref[slot], NN)
    part[...] = total
    greet(rows, cols, c, sends)
    copies = exchange_start(part, slots, ex_send, ex_recv, cols)
    for copy in copies:
        copy.wait()
    total = part[...]
    for step in range(cols - 1):
        total = total + slots[step]
    own_ref[...] = total

    @pl.when(sends)
    def _():
        spread(own_ref, image_ref, slot_own, rows, c, send_sem, recv_sem, False)
        image_ref[slot_own] = total

    mid[...] = jnp.zeros_like(mid)

    def mid_step(slot, carry):
        @pl.when(slot * cols + c != r)
        def _():
            arrive(own_ref, image_ref, slot, recv_sem)

        mid[...] += product(vec_ref[slot], image_ref[slot], TN)
        return carry

    lax.fori_loop(0, count, mid_step, 0)
    copies = exchange_start(mid, mid_slots, mid_send, mid_recv, cols)
    for copy in copies:
        copy.wait()
    total = mid[...]
    for step in range(cols - 1):
        total = total + mid_slots[step]
    middle_ref[...] = total

    @pl.when(sends)
    def _():
        spread(own_ref, image_ref, slot_own, rows, c, send_sem, recv_sem, True)


def vmem(count):
    return [pl.BlockSpec(memory_space=pltpu.VMEM)] * count


def f32(*shape):
    return jax.ShapeDtypeStruct(shape, jnp.float32)


def gather_panel(matrix, rows, cols):
    _, width, count, _ = matrix.shape
    dma = pltpu.SemaphoreType.DMA
    return pl.pallas_call(
        functools.partial(gather_kernel, rows, cols),
        out_shape=(f32(count, width, width), f32(width, width), f32(2, width, width)),
        in_specs=vmem(1),
        out_specs=tuple(vmem(3)),
        scratch_shapes=[
            pltpu.VMEM((2, width, width), jnp.float32),
            pltpu.VMEM((cols - 1, 2, width, width), jnp.float32),
            dma((rows,)), dma((count,)), dma((cols - 1,)), dma,
            dma((cols - 1,)), dma((cols - 1,)),
        ],
        compiler_params=pltpu.CompilerParams(
            collective_id=0, has_side_effects=True, vmem_limit_bytes=VMEM_LIMIT
        ),
    )(matrix)


def gather_image(matrix, vectors, rows, cols):
    _, width, count, _ = matrix.shape
    dma = pltpu.SemaphoreType.DMA
    return pl.pallas_call(
        functools.partial(image_kernel, rows, cols),
        out_shape=(f32(count, width, width), f32(width, width), f32(width, width)),
        in_specs=vmem(2),
        out_specs=tuple(vmem(3)),
        scratch_shapes=[
            pltpu.VMEM((width, width), jnp.float32),
            pltpu.VMEM((cols - 1, width, width), jnp.float32),
            pltpu.VMEM((width, width), jnp.float32),
            pltpu.VMEM((cols - 1, width, width), jnp.float32),
            dma((rows,)), dma((count,)), dma((cols - 1,)), dma((cols - 1,)),
            dma((cols - 1,)), dma((cols - 1,)),
        ],
        compiler_params=pltpu.CompilerParams(
            collective_id=1, has_side_effects=True, vmem_limit_bytes=VMEM_LIMIT
        ),
    )(matrix, vectors)


def per_device(matrix):
    _, width, count, _ = matrix.shape
    rows = lax.axis_size("row")
    cols = lax.axis_size("col")
    r = lax.axis_index("row")
    c = lax.axis_index("col")
    col_tiles = jnp.arange(count, dtype=jnp.int32) * cols + c
    identity = jnp.eye(width, dtype=jnp.float32)
    tiles, own, sums = gather_panel(matrix, rows, cols)
    gram, head = sums[0], sums[1]
    lower = jnp.linalg.cholesky(gram)
    inverse = jax.scipy.linalg.solve_triangular(lower, identity, lower=True)
    shifted = identity + product(inverse, head, NT)
    normal = product(shifted, shifted, TN)
    coupling = jax.scipy.linalg.cho_solve((jnp.linalg.cholesky(normal), True), shifted.T)
    row_vec = jnp.where(r != 0, product(own, inverse, NT), 0.0) + jnp.where(r == 1, identity, 0.0)
    col_vec = product(tiles.reshape(count * width, width), inverse, NT).reshape(tiles.shape)
    col_vec = jnp.where((col_tiles != 0)[:, None, None], col_vec, 0.0) + jnp.where(
        (col_tiles == 1)[:, None, None], identity, 0.0
    )
    image, own_image, middle = gather_image(matrix, col_vec, rows, cols)
    sandwich = product(coupling, product(middle, coupling, NN), TN)
    flat_vec = col_vec.reshape(count * width, width)
    flat_image = image.reshape(count * width, width)
    upd_rows = product(own_image, coupling, NN) - 0.5 * product(row_vec, sandwich, NN)
    upd_cols = product(flat_image, coupling, NN) - 0.5 * product(flat_vec, sandwich, NN)
    left = jnp.concatenate([upd_rows, row_vec], axis=1)
    right = jnp.concatenate([flat_vec, upd_cols], axis=1)
    change = product(left, right, NT)
    return matrix - change.reshape(matrix.shape)


def solution(mesh):
    in_specs = (P(None, "row", None, "col"),)
    out_specs = P(None, "row", None, "col")
    return jax.shard_map(
        per_device, mesh=mesh, in_specs=in_specs, out_specs=out_specs, check_vma=False
    )
```

```python
import functools

import jax
import jax.numpy as jnp
from jax import lax
from jax.experimental import pallas as pl
from jax.experimental.pallas import tpu as pltpu
from jax.sharding import PartitionSpec as P

MESH = pl.DeviceIdType.MESH
VMEM_LIMIT = 48 * 1024 * 1024


def product(left, right, contract):
    return lax.dot_general(
        left,
        right,
        (contract, ((), ())),
        precision=lax.Precision.HIGHEST,
        preferred_element_type=jnp.float32,
    )


TN = ((0,), (0,))
NN = ((1,), (0,))
NT = ((1,), (1,))


def exchange_start(source, slots, send_sem, recv_sem, cols):
    c = lax.axis_index("col")
    r = lax.axis_index("row")
    copies = []
    for step in range(1, cols):
        copy = pltpu.make_async_remote_copy(
            src_ref=source,
            dst_ref=slots.at[step - 1],
            send_sem=send_sem.at[step - 1],
            recv_sem=recv_sem.at[step - 1],
            device_id=(r, lax.rem(c + step, cols)),
            device_id_type=MESH,
        )
        copy.start()
        copies.append(copy)
    return copies


def spread(source, dest, slot, rows, target_col, send_sem, recv_sem, wait):
    r = lax.axis_index("row")

    def body(step, carry):
        copy = pltpu.make_async_remote_copy(
            src_ref=source,
            dst_ref=dest.at[slot],
            send_sem=send_sem.at[step],
            recv_sem=recv_sem.at[slot],
            device_id=(lax.rem(r + step, rows), target_col),
            device_id_type=MESH,
        )
        if wait:
            copy.wait_send()
        else:
            copy.start()
        return carry

    lax.fori_loop(1, rows, body, 0)


def arrive(source, dest, slot, recv_sem):
    pltpu.make_async_remote_copy(
        src_ref=source,
        dst_ref=dest.at[slot],
        send_sem=recv_sem.at[slot],
        recv_sem=recv_sem.at[slot],
        device_id=(lax.axis_index("row"), lax.axis_index("col")),
        device_id_type=MESH,
    ).wait_recv()


def greet(rows, cols, root_col, sends):
    r = lax.axis_index("row")
    c = lax.axis_index("col")
    barrier = pltpu.get_barrier_semaphore()

    def body(slot, carry):
        root = slot * cols + c

        @pl.when(root != r)
        def _():
            pl.semaphore_signal(barrier, inc=1, device_id=(root, root_col), device_id_type=MESH)

        return carry

    lax.fori_loop(0, rows // cols, body, 0)
    for step in range(1, cols):
        pl.semaphore_signal(
            barrier, inc=1, device_id=(r, lax.rem(c + step, cols)), device_id_type=MESH
        )

    @pl.when(sends)
    def _():
        pl.semaphore_wait(barrier, rows - 1 + cols - 1)

    @pl.when(jnp.logical_not(sends))
    def _():
        pl.semaphore_wait(barrier, cols - 1)


def gather_kernel(
    rows, cols, local_ref, tiles_ref, own_ref, sums_ref,
    parts, slots, send_sem, recv_sem, own_send, own_recv, ex_send, ex_recv,
):
    r = lax.axis_index("row")
    c = lax.axis_index("col")
    is_root = c == 0
    count = rows // cols
    slot_own = r // cols
    own_col = lax.rem(r, cols)

    @pl.when(is_root)
    def _():
        own_ref[...] = local_ref[0, :, 0, :]

    greet(rows, cols, 0, is_root)

    @pl.when(is_root)
    def _():
        for peer in range(1, cols):
            pltpu.make_async_remote_copy(
                src_ref=own_ref, dst_ref=own_ref, send_sem=own_send.at[peer - 1],
                recv_sem=own_recv, device_id=(r, peer), device_id_type=MESH,
            ).start()
        spread(own_ref, tiles_ref, slot_own, rows, own_col, send_sem, recv_sem, False)

    @pl.when(jnp.logical_not(is_root))
    def _():
        pltpu.make_async_remote_copy(
            src_ref=own_ref, dst_ref=own_ref, send_sem=own_recv,
            recv_sem=own_recv, device_id=(r, c), device_id_type=MESH,
        ).wait_recv()

    @pl.when(own_col == c)
    def _():
        tiles_ref[slot_own] = own_ref[...]

    parts[...] = jnp.zeros_like(parts)

    def gram_step(slot, carry):
        tile = slot * cols + c

        @pl.when(tile != r)
        def _():
            arrive(own_ref, tiles_ref, slot, recv_sem)

        @pl.when(tile != 0)
        def _():
            block = tiles_ref[slot]
            parts[0] += product(block, block, TN)

        @pl.when(tile == 1)
        def _():
            parts[1] = tiles_ref[slot]

        return carry

    lax.fori_loop(0, count, gram_step, 0)
    copies = exchange_start(parts, slots, ex_send, ex_recv, cols)
    for copy in copies:
        copy.wait()
    total = parts[...]
    for step in range(cols - 1):
        total = total + slots[step]
    sums_ref[...] = total

    @pl.when(is_root)
    def _():
        for peer in range(1, cols):
            pltpu.make_async_remote_copy(
                src_ref=own_ref, dst_ref=own_ref, send_sem=own_send.at[peer - 1],
                recv_sem=own_recv, device_id=(r, peer), device_id_type=MESH,
            ).wait_send()
        spread(own_ref, tiles_ref, slot_own, rows, own_col, send_sem, recv_sem, True)


def image_kernel(
    rows, cols, local_ref, vec_ref, image_ref, own_ref, middle_ref,
    part, slots, mid, mid_slots, send_sem, recv_sem, ex_send, ex_recv, mid_send, mid_recv,
):
    r = lax.axis_index("row")
    c = lax.axis_index("col")
    count = rows // cols
    slot_own = r // cols
    sends = lax.rem(r, cols) == c
    total = product(local_ref[0, :, 0, :], vec_ref[0], NN)
    for slot in range(1, count):
        total = total + product(local_ref[0, :, slot, :], vec_ref[slot], NN)
    part[...] = total
    greet(rows, cols, c, sends)
    copies = exchange_start(part, slots, ex_send, ex_recv, cols)
    for copy in copies:
        copy.wait()
    total = part[...]
    for step in range(cols - 1):
        total = total + slots[step]
    own_ref[...] = total

    @pl.when(sends)
    def _():
        spread(own_ref, image_ref, slot_own, rows, c, send_sem, recv_sem, False)
        image_ref[slot_own] = total

    mid[...] = jnp.zeros_like(mid)

    def mid_step(slot, carry):
        @pl.when(slot * cols + c != r)
        def _():
            arrive(own_ref, image_ref, slot, recv_sem)

        mid[...] += product(vec_ref[slot], image_ref[slot], TN)
        return carry

    lax.fori_loop(0, count, mid_step, 0)
    copies = exchange_start(mid, mid_slots, mid_send, mid_recv, cols)
    for copy in copies:
        copy.wait()
    total = mid[...]
    for step in range(cols - 1):
        total = total + mid_slots[step]
    middle_ref[...] = total

    @pl.when(sends)
    def _():
        spread(own_ref, image_ref, slot_own, rows, c, send_sem, recv_sem, True)


BLOCK = 16


def columns_of(block):
    size, lanes = block.shape[0], 128
    return [jnp.broadcast_to(block[:, j : j + 1], (size, lanes)) for j in range(size)]


def small_cholesky_inverse(block):
    size = block.shape[0]
    cols = columns_of(block)
    row = lax.broadcasted_iota(jnp.int32, (size, 128), 0)
    lane = lax.broadcasted_iota(jnp.int32, (size, 128), 1)
    inv = (row == lane).astype(jnp.float32)
    for j in range(size):
        scale = lax.rsqrt(cols[j][j : j + 1])
        factor = cols[j] * scale
        for k in range(j + 1, size):
            cols[k] = cols[k] - factor * factor[k : k + 1]
        pivot = inv[j : j + 1] * scale
        below = jnp.where(row > j, factor, 0.0)
        inv = jnp.where(row == j, pivot, inv - below * pivot)
    return inv[:, :size]


def small_inverse(block):
    size = block.shape[0]
    cols = columns_of(block)
    row = lax.broadcasted_iota(jnp.int32, (size, 128), 0)
    lane = lax.broadcasted_iota(jnp.int32, (size, 128), 1)
    inv = (row == lane).astype(jnp.float32)
    for j in range(size):
        scale = 1.0 / cols[j][j : j + 1]
        others = jnp.where(row == j, 0.0, cols[j])
        for k in range(j + 1, size):
            pivot = cols[k][j : j + 1] * scale
            cols[k] = jnp.where(row == j, pivot, cols[k] - others * pivot)
        pivot = inv[j : j + 1] * scale
        inv = jnp.where(row == j, pivot, inv - others * pivot)
    return inv[:, :size]


def unit(width):
    row = lax.broadcasted_iota(jnp.int32, (width, width), 0)
    lane = lax.broadcasted_iota(jnp.int32, (width, width), 1)
    return (row == lane).astype(jnp.float32)


def cholesky_inverse(gram):
    width = gram.shape[0]
    step = min(BLOCK, width)
    rest = jnp.concatenate([gram, unit(width)], axis=1)
    done = []
    for start in range(0, width, step):
        small = small_cholesky_inverse(rest[:step, start : start + step])
        lead = product(small, rest[:step], NN)
        done.append(lead[:, width:])
        if start + step < width:
            rest = rest[step:] - product(lead[:, start + step : width], lead, TN)
    return jnp.concatenate(done, axis=0)


def full_inverse(matrix):
    width = matrix.shape[0]
    step = min(BLOCK, width)
    work = jnp.concatenate([matrix, unit(width)], axis=1)
    row = lax.broadcasted_iota(jnp.int32, (width, step), 0)
    for start in range(0, width, step):
        stop = start + step
        small = small_inverse(work[start:stop, start:stop])
        lead = product(small, work[start:stop], NN)
        inside = jnp.logical_and(row >= start, row < stop)
        work = work - product(jnp.where(inside, 0.0, work[:, start:stop]), lead, NN)
        pieces = [work[:start], lead, work[stop:]]
        work = jnp.concatenate([piece for piece in pieces if piece.shape[0]], axis=0)
    return work[:, width:]


def factor_kernel(rows, cols, sums_ref, own_ref, tiles_ref, row_ref, vec_ref, coupling_ref):
    r = lax.axis_index("row")
    c = lax.axis_index("col")
    width = own_ref.shape[0]
    identity = unit(width)
    inverse = cholesky_inverse(sums_ref[0])

    def vectors(tile, block):
        keep = (tile != 0).astype(jnp.float32)
        first = (tile == 1).astype(jnp.float32)
        return product(block, inverse, NT) * keep + identity * first

    row_ref[...] = vectors(r, own_ref[...])
    for slot in range(rows // cols):
        vec_ref[slot] = vectors(slot * cols + c, tiles_ref[slot])
    coupling_ref[...] = full_inverse(identity + product(inverse, sums_ref[1], NT))


def vmem(count):
    return [pl.BlockSpec(memory_space=pltpu.VMEM)] * count


def f32(*shape):
    return jax.ShapeDtypeStruct(shape, jnp.float32)


def gather_panel(matrix, rows, cols):
    _, width, count, _ = matrix.shape
    dma = pltpu.SemaphoreType.DMA
    return pl.pallas_call(
        functools.partial(gather_kernel, rows, cols),
        out_shape=(f32(count, width, width), f32(width, width), f32(2, width, width)),
        in_specs=vmem(1),
        out_specs=tuple(vmem(3)),
        scratch_shapes=[
            pltpu.VMEM((2, width, width), jnp.float32),
            pltpu.VMEM((cols - 1, 2, width, width), jnp.float32),
            dma((rows,)), dma((count,)), dma((cols - 1,)), dma,
            dma((cols - 1,)), dma((cols - 1,)),
        ],
        compiler_params=pltpu.CompilerParams(
            collective_id=0, has_side_effects=True, vmem_limit_bytes=VMEM_LIMIT
        ),
    )(matrix)


def gather_image(matrix, vectors, rows, cols):
    _, width, count, _ = matrix.shape
    dma = pltpu.SemaphoreType.DMA
    return pl.pallas_call(
        functools.partial(image_kernel, rows, cols),
        out_shape=(f32(count, width, width), f32(width, width), f32(width, width)),
        in_specs=vmem(2),
        out_specs=tuple(vmem(3)),
        scratch_shapes=[
            pltpu.VMEM((width, width), jnp.float32),
            pltpu.VMEM((cols - 1, width, width), jnp.float32),
            pltpu.VMEM((width, width), jnp.float32),
            pltpu.VMEM((cols - 1, width, width), jnp.float32),
            dma((rows,)), dma((count,)), dma((cols - 1,)), dma((cols - 1,)),
            dma((cols - 1,)), dma((cols - 1,)),
        ],
        compiler_params=pltpu.CompilerParams(
            collective_id=1, has_side_effects=True, vmem_limit_bytes=VMEM_LIMIT
        ),
    )(matrix, vectors)


def factor(sums, own, tiles, rows, cols):
    width = own.shape[0]
    return pl.pallas_call(
        functools.partial(factor_kernel, rows, cols),
        out_shape=(f32(width, width), f32(*tiles.shape), f32(width, width)),
        in_specs=vmem(3),
        out_specs=tuple(vmem(3)),
        compiler_params=pltpu.CompilerParams(vmem_limit_bytes=VMEM_LIMIT),
    )(sums, own, tiles)


def per_device(matrix):
    _, width, count, _ = matrix.shape
    rows = lax.axis_size("row")
    cols = lax.axis_size("col")
    tiles, own, sums = gather_panel(matrix, rows, cols)
    row_vec, col_vec, coupling = factor(sums, own, tiles, rows, cols)
    image, own_image, middle = gather_image(matrix, col_vec, rows, cols)
    sandwich = product(coupling, product(middle, coupling, NN), TN)
    flat_vec = col_vec.reshape(count * width, width)
    flat_image = image.reshape(count * width, width)
    upd_rows = product(own_image, coupling, NN) - 0.5 * product(row_vec, sandwich, NN)
    upd_cols = product(flat_image, coupling, NN) - 0.5 * product(flat_vec, sandwich, NN)
    left = jnp.concatenate([upd_rows, row_vec], axis=1)
    right = jnp.concatenate([flat_vec, upd_cols], axis=1)
    change = product(left, right, NT)
    return matrix - change.reshape(matrix.shape)


def solution(mesh):
    in_specs = (P(None, "row", None, "col"),)
    out_specs = P(None, "row", None, "col")
    return jax.shard_map(
        per_device, mesh=mesh, in_specs=in_specs, out_specs=out_specs, check_vma=False
    )
```

```python
import functools

import jax
import jax.numpy as jnp
from jax import lax
from jax.experimental import pallas as pl
from jax.experimental.pallas import tpu as pltpu
from jax.sharding import PartitionSpec as P

MESH = pl.DeviceIdType.MESH
VMEM_LIMIT = 48 * 1024 * 1024


def product(left, right, contract):
    return lax.dot_general(
        left,
        right,
        (contract, ((), ())),
        precision=lax.Precision.HIGHEST,
        preferred_element_type=jnp.float32,
    )


TN = ((0,), (0,))
NN = ((1,), (0,))
NT = ((1,), (1,))


def exchange_start(source, slots, send_sem, recv_sem, cols):
    c = lax.axis_index("col")
    r = lax.axis_index("row")
    copies = []
    for step in range(1, cols):
        copy = pltpu.make_async_remote_copy(
            src_ref=source,
            dst_ref=slots.at[step - 1],
            send_sem=send_sem.at[step - 1],
            recv_sem=recv_sem.at[step - 1],
            device_id=(r, lax.rem(c + step, cols)),
            device_id_type=MESH,
        )
        copy.start()
        copies.append(copy)
    return copies


def spread(source, dest, slot, rows, target_col, send_sem, recv_sem, wait):
    r = lax.axis_index("row")

    def body(step, carry):
        copy = pltpu.make_async_remote_copy(
            src_ref=source,
            dst_ref=dest.at[slot],
            send_sem=send_sem.at[step],
            recv_sem=recv_sem.at[slot],
            device_id=(lax.rem(r + step, rows), target_col),
            device_id_type=MESH,
        )
        if wait:
            copy.wait_send()
        else:
            copy.start()
        return carry

    lax.fori_loop(1, rows, body, 0)


def arrive(source, dest, slot, recv_sem):
    pltpu.make_async_remote_copy(
        src_ref=source,
        dst_ref=dest.at[slot],
        send_sem=recv_sem.at[slot],
        recv_sem=recv_sem.at[slot],
        device_id=(lax.axis_index("row"), lax.axis_index("col")),
        device_id_type=MESH,
    ).wait_recv()


BLOCK = 16


def columns_of(block):
    size, lanes = block.shape[0], 128
    return [jnp.broadcast_to(block[:, j : j + 1], (size, lanes)) for j in range(size)]


def small_cholesky_inverse(block):
    size = block.shape[0]
    cols = columns_of(block)
    row = lax.broadcasted_iota(jnp.int32, (size, 128), 0)
    lane = lax.broadcasted_iota(jnp.int32, (size, 128), 1)
    inv = (row == lane).astype(jnp.float32)
    for j in range(size):
        scale = lax.rsqrt(cols[j][j : j + 1])
        factor = cols[j] * scale
        for k in range(j + 1, size):
            cols[k] = cols[k] - factor * factor[k : k + 1]
        pivot = inv[j : j + 1] * scale
        below = jnp.where(row > j, factor, 0.0)
        inv = jnp.where(row == j, pivot, inv - below * pivot)
    return inv[:, :size]


def small_inverse(block):
    size = block.shape[0]
    cols = columns_of(block)
    row = lax.broadcasted_iota(jnp.int32, (size, 128), 0)
    lane = lax.broadcasted_iota(jnp.int32, (size, 128), 1)
    inv = (row == lane).astype(jnp.float32)
    for j in range(size):
        scale = 1.0 / cols[j][j : j + 1]
        others = jnp.where(row == j, 0.0, cols[j])
        for k in range(j + 1, size):
            pivot = cols[k][j : j + 1] * scale
            cols[k] = jnp.where(row == j, pivot, cols[k] - others * pivot)
        pivot = inv[j : j + 1] * scale
        inv = jnp.where(row == j, pivot, inv - others * pivot)
    return inv[:, :size]


def unit(width):
    row = lax.broadcasted_iota(jnp.int32, (width, width), 0)
    lane = lax.broadcasted_iota(jnp.int32, (width, width), 1)
    return (row == lane).astype(jnp.float32)


def cholesky_inverse(gram):
    width = gram.shape[0]
    step = min(BLOCK, width)
    rest = jnp.concatenate([gram, unit(width)], axis=1)
    done = []
    for start in range(0, width, step):
        small = small_cholesky_inverse(rest[:step, start : start + step])
        lead = product(small, rest[:step], NN)
        done.append(lead[:, width:])
        if start + step < width:
            rest = rest[step:] - product(lead[:, start + step : width], lead, TN)
    return jnp.concatenate(done, axis=0)


def full_inverse(matrix):
    width = matrix.shape[0]
    step = min(BLOCK, width)
    work = jnp.concatenate([matrix, unit(width)], axis=1)
    row = lax.broadcasted_iota(jnp.int32, (width, step), 0)
    for start in range(0, width, step):
        stop = start + step
        small = small_inverse(work[start:stop, start:stop])
        lead = product(small, work[start:stop], NN)
        inside = jnp.logical_and(row >= start, row < stop)
        work = work - product(jnp.where(inside, 0.0, work[:, start:stop]), lead, NN)
        pieces = [work[:start], lead, work[stop:]]
        work = jnp.concatenate([piece for piece in pieces if piece.shape[0]], axis=0)
    return work[:, width:]


def greet(rows, cols):
    r = lax.axis_index("row")
    c = lax.axis_index("col")
    barrier = pltpu.get_barrier_semaphore()

    def body(slot, carry):
        root = slot * cols + c

        @pl.when(root != r)
        def _():
            pl.semaphore_signal(barrier, inc=1, device_id=(root, 0), device_id_type=MESH)

        @pl.when(jnp.logical_and(root != r, c != 0))
        def _():
            pl.semaphore_signal(barrier, inc=1, device_id=(root, c), device_id_type=MESH)

        return carry

    lax.fori_loop(0, rows // cols, body, 0)
    for step in range(1, cols):
        pl.semaphore_signal(
            barrier, inc=1, device_id=(r, lax.rem(c + step, cols)), device_id_type=MESH
        )


def greeted(rows, cols, sends):
    barrier = pltpu.get_barrier_semaphore()

    @pl.when(sends)
    def _():
        pl.semaphore_wait(barrier, rows - 1 + cols - 1)

    @pl.when(jnp.logical_not(sends))
    def _():
        pl.semaphore_wait(barrier, cols - 1)


def split(value):
    high = value.astype(jnp.bfloat16)
    return high, (value - high.astype(jnp.float32)).astype(jnp.bfloat16)


def product3(left, right, contract):
    def one(a, b):
        return lax.dot_general(a, b, (contract, ((), ())), preferred_element_type=jnp.float32)

    return one(left[0], right[0]) + (one(left[0], right[1]) + one(left[1], right[0]))


def panel_kernel(
    rows, cols, local_ref, change_ref,
    tiles, own, parts, slots, vecs, image, own_image, part_slots, mid, mid_slots, wide_high, wide_low,
    send_sem, recv_sem, own_send, own_recv, ex_send, ex_recv,
    im_send, im_recv, part_send, part_recv, mid_send, mid_recv,
):
    r = lax.axis_index("row")
    c = lax.axis_index("col")
    width = own.shape[0]
    is_root = c == 0
    count = rows // cols
    slot_own = r // cols
    own_col = lax.rem(r, cols)
    sends = own_col == c
    identity = unit(width)
    greet(rows, cols)

    @pl.when(is_root)
    def _():
        own[...] = local_ref[0, :, 0, :]

    greeted(rows, cols, jnp.logical_or(is_root, sends))

    @pl.when(is_root)
    def _():
        for peer in range(1, cols):
            pltpu.make_async_remote_copy(
                src_ref=own, dst_ref=own, send_sem=own_send.at[peer - 1],
                recv_sem=own_recv, device_id=(r, peer), device_id_type=MESH,
            ).start()
        spread(own, tiles, slot_own, rows, own_col, send_sem, recv_sem, False)

    for slot in range(count):
        columns = slice(slot * width, slot * width + width)
        wide_high[:, columns], wide_low[:, columns] = split(local_ref[0, :, slot, :])

    @pl.when(jnp.logical_not(is_root))
    def _():
        pltpu.make_async_remote_copy(
            src_ref=own, dst_ref=own, send_sem=own_recv,
            recv_sem=own_recv, device_id=(r, c), device_id_type=MESH,
        ).wait_recv()

    @pl.when(sends)
    def _():
        tiles[slot_own] = own[...]

    parts[...] = jnp.zeros_like(parts)

    def gram_step(slot, carry):
        tile = slot * cols + c

        @pl.when(tile != r)
        def _():
            arrive(own, tiles, slot, recv_sem)

        @pl.when(tile != 0)
        def _():
            block = tiles[slot]
            parts[0] += product(block, block, TN)

        @pl.when(tile == 1)
        def _():
            parts[1] = tiles[slot]

        return carry

    lax.fori_loop(0, count, gram_step, 0)
    for copy in exchange_start(parts, slots, ex_send, ex_recv, cols):
        copy.wait()
    sums = parts[...]
    for step in range(cols - 1):
        sums = sums + slots[step]
    inverse = cholesky_inverse(sums[0])

    def vectors(tile, block):
        keep = (tile != 0).astype(jnp.float32)
        first = (tile == 1).astype(jnp.float32)
        return product(block, inverse, NT) * keep + identity * first

    for slot in range(count):
        vecs[slot] = vectors(slot * cols + c, tiles[slot])
    flat_vec = vecs[...].reshape(count * width, width)
    vec_parts = split(flat_vec)
    mid[...] = product3((wide_high[...], wide_low[...]), vec_parts, NN)
    copies = exchange_start(mid, part_slots, part_send, part_recv, cols)
    row_vec = vectors(r, own[...])
    for copy in copies:
        copy.wait()
    total = mid[...]
    for step in range(cols - 1):
        total = total + part_slots[step]
    own_image[...] = total

    @pl.when(sends)
    def _():
        spread(own_image, image, slot_own, rows, c, im_send, im_recv, False)
        image[slot_own] = total

    coupling = full_inverse(identity + product(inverse, sums[1], NT))
    upd_rows = product(total, coupling, NN)

    mid[...] = jnp.zeros_like(mid)

    def mid_step(slot, carry):
        @pl.when(slot * cols + c != r)
        def _():
            arrive(own_image, image, slot, im_recv)

        mid[...] += product(vecs[slot], image[slot], TN)
        return carry

    lax.fori_loop(0, count, mid_step, 0)
    copies = exchange_start(mid, mid_slots, mid_send, mid_recv, cols)
    upd_cols = product3(split(image[...].reshape(count * width, width)), split(coupling), NN)
    for copy in copies:
        copy.wait()
    middle = mid[...]
    for step in range(cols - 1):
        middle = middle + mid_slots[step]
    half = 0.5 * product(coupling, product(middle, coupling, NN), TN)
    upd_rows = upd_rows - product(row_vec, half, NN)
    upd_cols = upd_cols - product3(vec_parts, split(half), NN)
    left = split(jnp.concatenate([upd_rows, row_vec], axis=1))
    right = split(jnp.concatenate([flat_vec, upd_cols], axis=1))
    change_ref[...] = product3(left, right, NT)

    @pl.when(is_root)
    def _():
        for peer in range(1, cols):
            pltpu.make_async_remote_copy(
                src_ref=own, dst_ref=own, send_sem=own_send.at[peer - 1],
                recv_sem=own_recv, device_id=(r, peer), device_id_type=MESH,
            ).wait_send()
        spread(own, tiles, slot_own, rows, own_col, send_sem, recv_sem, True)

    @pl.when(sends)
    def _():
        spread(own_image, image, slot_own, rows, c, im_send, im_recv, True)


def per_device(matrix):
    _, width, count, _ = matrix.shape
    rows = lax.axis_size("row")
    cols = lax.axis_size("col")
    dma = pltpu.SemaphoreType.DMA

    def buffer(*shape):
        return pltpu.VMEM((*shape, width, width), jnp.float32)

    change = pl.pallas_call(
        functools.partial(panel_kernel, rows, cols),
        out_shape=jax.ShapeDtypeStruct((width, count * width), jnp.float32),
        in_specs=[pl.BlockSpec(memory_space=pltpu.VMEM)],
        out_specs=pl.BlockSpec(memory_space=pltpu.VMEM),
        scratch_shapes=[
            buffer(count), buffer(), buffer(2), buffer(cols - 1, 2), buffer(count), buffer(count),
            buffer(), buffer(cols - 1), buffer(), buffer(cols - 1),
            pltpu.VMEM((width, count * width), jnp.bfloat16),
            pltpu.VMEM((width, count * width), jnp.bfloat16),
            dma((rows,)), dma((count,)), dma((cols - 1,)), dma, dma((cols - 1,)), dma((cols - 1,)),
            dma((rows,)), dma((count,)), dma((cols - 1,)), dma((cols - 1,)),
            dma((cols - 1,)), dma((cols - 1,)),
        ],
        compiler_params=pltpu.CompilerParams(
            collective_id=0, has_side_effects=True, vmem_limit_bytes=VMEM_LIMIT
        ),
    )(matrix)
    return matrix - change.reshape(matrix.shape)


def solution(mesh):
    in_specs = (P(None, "row", None, "col"),)
    out_specs = P(None, "row", None, "col")
    return jax.shard_map(
        per_device, mesh=mesh, in_specs=in_specs, out_specs=out_specs, check_vma=False
    )
```

```python
import functools

import jax
import jax.numpy as jnp
from jax import lax
from jax.experimental import pallas as pl
from jax.experimental.pallas import tpu as pltpu
from jax.sharding import PartitionSpec as P

MESH = pl.DeviceIdType.MESH
VMEM_LIMIT = 48 * 1024 * 1024


def product(left, right, contract):
    return lax.dot_general(
        left,
        right,
        (contract, ((), ())),
        precision=lax.Precision.HIGHEST,
        preferred_element_type=jnp.float32,
    )


TN = ((0,), (0,))
NN = ((1,), (0,))
NT = ((1,), (1,))


def exchange_start(source, slots, send_sem, recv_sem, cols):
    c = lax.axis_index("col")
    r = lax.axis_index("row")
    copies = []
    for step in range(1, cols):
        copy = pltpu.make_async_remote_copy(
            src_ref=source,
            dst_ref=slots.at[step - 1],
            send_sem=send_sem.at[step - 1],
            recv_sem=recv_sem.at[step - 1],
            device_id=(r, lax.rem(c + step, cols)),
            device_id_type=MESH,
        )
        copy.start()
        copies.append(copy)
    return copies


def plane_of(rows, cols):
    plane = cols
    while plane * plane < rows or rows % plane:
        plane += cols
    return plane


def across(source, dest, rows, cols, target_col, send_sem, recv_sem, wait):
    r = lax.axis_index("row")
    plane = plane_of(rows, cols)

    def body(step, carry):
        copy = pltpu.make_async_remote_copy(
            src_ref=source,
            dst_ref=dest.at[r // cols],
            send_sem=send_sem.at[step * plane],
            recv_sem=recv_sem.at[r // cols],
            device_id=(lax.rem(r + step * plane, rows), target_col),
            device_id_type=MESH,
        )
        if wait:
            copy.wait_send()
        else:
            copy.start()
        return carry

    lax.fori_loop(1, rows // plane, body, 0)


def within(source, dest, rows, cols, send_sem, recv_sem, wait):
    r = lax.axis_index("row")
    c = lax.axis_index("col")
    plane = plane_of(rows, cols)
    base = (r // plane) * plane
    place = lax.rem(r, plane)

    def body(step, carry):
        slot = lax.rem(r + step * plane, rows) // cols
        if not wait:

            @pl.when(step > 0)
            def _():
                arrive(source, dest, slot, recv_sem)

        for other in range(1, plane):
            copy = pltpu.make_async_remote_copy(
                src_ref=dest.at[slot],
                dst_ref=dest.at[slot],
                send_sem=send_sem.at[step * plane + other],
                recv_sem=recv_sem.at[slot],
                device_id=(base + lax.rem(place + other, plane), c),
                device_id_type=MESH,
            )
            if wait:
                copy.wait_send()
            else:
                copy.start()
        return carry

    lax.fori_loop(0, rows // plane, body, 0)


def arrive(source, dest, slot, recv_sem):
    pltpu.make_async_remote_copy(
        src_ref=source,
        dst_ref=dest.at[slot],
        send_sem=recv_sem.at[slot],
        recv_sem=recv_sem.at[slot],
        device_id=(lax.axis_index("row"), lax.axis_index("col")),
        device_id_type=MESH,
    ).wait_recv()


BLOCK = 16


def columns_of(block):
    size, lanes = block.shape[0], 128
    return [jnp.broadcast_to(block[:, j : j + 1], (size, lanes)) for j in range(size)]


def small_cholesky_inverse(block):
    size = block.shape[0]
    cols = columns_of(block)
    row = lax.broadcasted_iota(jnp.int32, (size, 128), 0)
    lane = lax.broadcasted_iota(jnp.int32, (size, 128), 1)
    inv = (row == lane).astype(jnp.float32)
    for j in range(size):
        scale = lax.rsqrt(cols[j][j : j + 1])
        factor = cols[j] * scale
        for k in range(j + 1, size):
            cols[k] = cols[k] - factor * factor[k : k + 1]
        pivot = inv[j : j + 1] * scale
        below = jnp.where(row > j, factor, 0.0)
        inv = jnp.where(row == j, pivot, inv - below * pivot)
    return inv[:, :size]


def small_inverse(block):
    size = block.shape[0]
    cols = columns_of(block)
    row = lax.broadcasted_iota(jnp.int32, (size, 128), 0)
    lane = lax.broadcasted_iota(jnp.int32, (size, 128), 1)
    inv = (row == lane).astype(jnp.float32)
    for j in range(size):
        scale = 1.0 / cols[j][j : j + 1]
        others = jnp.where(row == j, 0.0, cols[j])
        for k in range(j + 1, size):
            pivot = cols[k][j : j + 1] * scale
            cols[k] = jnp.where(row == j, pivot, cols[k] - others * pivot)
        pivot = inv[j : j + 1] * scale
        inv = jnp.where(row == j, pivot, inv - others * pivot)
    return inv[:, :size]


def unit(width):
    row = lax.broadcasted_iota(jnp.int32, (width, width), 0)
    lane = lax.broadcasted_iota(jnp.int32, (width, width), 1)
    return (row == lane).astype(jnp.float32)


def cholesky_inverse(gram):
    width = gram.shape[0]
    step = min(BLOCK, width)
    rest = jnp.concatenate([gram, unit(width)], axis=1)
    done = []
    for start in range(0, width, step):
        small = small_cholesky_inverse(rest[:step, start : start + step])
        lead = product(small, rest[:step], NN)
        done.append(lead[:, width:])
        if start + step < width:
            rest = rest[step:] - product(lead[:, start + step : width], lead, TN)
    return jnp.concatenate(done, axis=0)


def full_inverse(matrix):
    width = matrix.shape[0]
    step = min(BLOCK, width)
    work = jnp.concatenate([matrix, unit(width)], axis=1)
    row = lax.broadcasted_iota(jnp.int32, (width, step), 0)
    for start in range(0, width, step):
        stop = start + step
        small = small_inverse(work[start:stop, start:stop])
        lead = product(small, work[start:stop], NN)
        inside = jnp.logical_and(row >= start, row < stop)
        work = work - product(jnp.where(inside, 0.0, work[:, start:stop]), lead, NN)
        pieces = [work[:start], lead, work[stop:]]
        work = jnp.concatenate([piece for piece in pieces if piece.shape[0]], axis=0)
    return work[:, width:]


def greet(rows, cols):
    r = lax.axis_index("row")
    c = lax.axis_index("col")
    barrier = pltpu.get_barrier_semaphore()
    plane = plane_of(rows, cols)
    base = (r // plane) * plane
    place = lax.rem(r, plane)

    @pl.when(lax.rem(r, cols) == c)
    def _():
        for step in range(1, rows // plane):
            root = lax.rem(r + step * plane, rows)
            pl.semaphore_signal(barrier, inc=1, device_id=(root, 0), device_id_type=MESH)

            @pl.when(c != 0)
            def _():
                pl.semaphore_signal(barrier, inc=1, device_id=(root, c), device_id_type=MESH)

    for index in range(plane // cols):
        other = index * cols + c

        @pl.when(other != place)
        def _():
            pl.semaphore_signal(barrier, inc=1, device_id=(base + other, c), device_id_type=MESH)

    for step in range(1, cols):
        pl.semaphore_signal(
            barrier, inc=1, device_id=(r, lax.rem(c + step, cols)), device_id_type=MESH
        )


def greeted(rows, cols, is_root, sends):
    barrier = pltpu.get_barrier_semaphore()
    plane = plane_of(rows, cols)
    outer = rows // plane - 1

    @pl.when(sends)
    def _():
        pl.semaphore_wait(barrier, outer + plane - 1 + cols - 1)

    @pl.when(jnp.logical_and(is_root, jnp.logical_not(sends)))
    def _():
        pl.semaphore_wait(barrier, outer + cols - 1)

    @pl.when(jnp.logical_not(jnp.logical_or(is_root, sends)))
    def _():
        pl.semaphore_wait(barrier, cols - 1)


def split(value):
    high = value.astype(jnp.bfloat16)
    return high, (value - high.astype(jnp.float32)).astype(jnp.bfloat16)


def product3(left, right, contract):
    def one(a, b):
        return lax.dot_general(a, b, (contract, ((), ())), preferred_element_type=jnp.float32)

    return one(left[0], right[0]) + (one(left[0], right[1]) + one(left[1], right[0]))


def panel_kernel(
    rows, cols, local_ref, change_ref,
    tiles, own, parts, slots, vecs, image, own_image, part_slots, mid, mid_slots, wide_high, wide_low,
    send_sem, recv_sem, own_send, own_recv, ex_send, ex_recv,
    im_send, im_recv, part_send, part_recv, mid_send, mid_recv,
):
    r = lax.axis_index("row")
    c = lax.axis_index("col")
    width = own.shape[0]
    is_root = c == 0
    count = rows // cols
    slot_own = r // cols
    own_col = lax.rem(r, cols)
    sends = own_col == c
    plane = plane_of(rows, cols)
    place = lax.rem(r, plane)
    identity = unit(width)
    greet(rows, cols)

    @pl.when(is_root)
    def _():
        own[...] = local_ref[0, :, 0, :]

    greeted(rows, cols, is_root, sends)

    @pl.when(is_root)
    def _():
        for peer in range(1, cols):
            pltpu.make_async_remote_copy(
                src_ref=own, dst_ref=own, send_sem=own_send.at[peer - 1],
                recv_sem=own_recv, device_id=(r, peer), device_id_type=MESH,
            ).start()
        across(own, tiles, rows, cols, own_col, send_sem, recv_sem, False)

    for slot in range(count):
        columns = slice(slot * width, slot * width + width)
        wide_high[:, columns], wide_low[:, columns] = split(local_ref[0, :, slot, :])

    @pl.when(jnp.logical_not(is_root))
    def _():
        pltpu.make_async_remote_copy(
            src_ref=own, dst_ref=own, send_sem=own_recv,
            recv_sem=own_recv, device_id=(r, c), device_id_type=MESH,
        ).wait_recv()

    @pl.when(sends)
    def _():
        tiles[slot_own] = own[...]
        within(own, tiles, rows, cols, send_sem, recv_sem, False)

    parts[...] = jnp.zeros_like(parts)

    def gram_step(slot, carry):
        tile = slot * cols + c

        @pl.when(jnp.logical_or(lax.rem(tile, plane) != place, jnp.logical_not(sends)))
        def _():
            arrive(own, tiles, slot, recv_sem)

        @pl.when(tile != 0)
        def _():
            block = tiles[slot]
            parts[0] += product(block, block, TN)

        @pl.when(tile == 1)
        def _():
            parts[1] = tiles[slot]

        return carry

    lax.fori_loop(0, count, gram_step, 0)
    for copy in exchange_start(parts, slots, ex_send, ex_recv, cols):
        copy.wait()
    sums = parts[...]
    for step in range(cols - 1):
        sums = sums + slots[step]
    inverse = cholesky_inverse(sums[0])

    def vectors(tile, block):
        keep = (tile != 0).astype(jnp.float32)
        first = (tile == 1).astype(jnp.float32)
        return product(block, inverse, NT) * keep + identity * first

    for slot in range(count):
        vecs[slot] = vectors(slot * cols + c, tiles[slot])
    flat_vec = vecs[...].reshape(count * width, width)
    vec_parts = split(flat_vec)
    mid[...] = product3((wide_high[...], wide_low[...]), vec_parts, NN)
    copies = exchange_start(mid, part_slots, part_send, part_recv, cols)
    row_vec = vectors(r, own[...])
    for copy in copies:
        copy.wait()
    total = mid[...]
    for step in range(cols - 1):
        total = total + part_slots[step]
    own_image[...] = total

    @pl.when(sends)
    def _():
        across(own_image, image, rows, cols, c, im_send, im_recv, False)
        image[slot_own] = total
        within(own_image, image, rows, cols, im_send, im_recv, False)

    coupling = full_inverse(identity + product(inverse, sums[1], NT))
    upd_rows = product(total, coupling, NN)

    mid[...] = jnp.zeros_like(mid)

    def mid_step(slot, carry):
        away = lax.rem(slot * cols + c, plane) != place

        @pl.when(jnp.logical_or(away, jnp.logical_not(sends)))
        def _():
            arrive(own_image, image, slot, im_recv)

        mid[...] += product(vecs[slot], image[slot], TN)
        return carry

    lax.fori_loop(0, count, mid_step, 0)
    copies = exchange_start(mid, mid_slots, mid_send, mid_recv, cols)
    upd_cols = product3(split(image[...].reshape(count * width, width)), split(coupling), NN)
    for copy in copies:
        copy.wait()
    middle = mid[...]
    for step in range(cols - 1):
        middle = middle + mid_slots[step]
    half = 0.5 * product(coupling, product(middle, coupling, NN), TN)
    upd_rows = upd_rows - product(row_vec, half, NN)
    upd_cols = upd_cols - product3(vec_parts, split(half), NN)
    left = split(jnp.concatenate([upd_rows, row_vec], axis=1))
    right = split(jnp.concatenate([flat_vec, upd_cols], axis=1))
    change_ref[...] = product3(left, right, NT)

    @pl.when(is_root)
    def _():
        for peer in range(1, cols):
            pltpu.make_async_remote_copy(
                src_ref=own, dst_ref=own, send_sem=own_send.at[peer - 1],
                recv_sem=own_recv, device_id=(r, peer), device_id_type=MESH,
            ).wait_send()
        across(own, tiles, rows, cols, own_col, send_sem, recv_sem, True)

    @pl.when(sends)
    def _():
        within(own, tiles, rows, cols, send_sem, recv_sem, True)
        across(own_image, image, rows, cols, c, im_send, im_recv, True)
        within(own_image, image, rows, cols, im_send, im_recv, True)


def per_device(matrix):
    _, width, count, _ = matrix.shape
    rows = lax.axis_size("row")
    cols = lax.axis_size("col")
    dma = pltpu.SemaphoreType.DMA

    def buffer(*shape):
        return pltpu.VMEM((*shape, width, width), jnp.float32)

    change = pl.pallas_call(
        functools.partial(panel_kernel, rows, cols),
        out_shape=jax.ShapeDtypeStruct((width, count * width), jnp.float32),
        in_specs=[pl.BlockSpec(memory_space=pltpu.VMEM)],
        out_specs=pl.BlockSpec(memory_space=pltpu.VMEM),
        scratch_shapes=[
            buffer(count), buffer(), buffer(2), buffer(cols - 1, 2), buffer(count), buffer(count),
            buffer(), buffer(cols - 1), buffer(), buffer(cols - 1),
            pltpu.VMEM((width, count * width), jnp.bfloat16),
            pltpu.VMEM((width, count * width), jnp.bfloat16),
            dma((rows,)), dma((count,)), dma((cols - 1,)), dma, dma((cols - 1,)), dma((cols - 1,)),
            dma((rows,)), dma((count,)), dma((cols - 1,)), dma((cols - 1,)),
            dma((cols - 1,)), dma((cols - 1,)),
        ],
        compiler_params=pltpu.CompilerParams(
            collective_id=0, has_side_effects=True, vmem_limit_bytes=VMEM_LIMIT
        ),
    )(matrix)
    return matrix - change.reshape(matrix.shape)


def solution(mesh):
    in_specs = (P(None, "row", None, "col"),)
    out_specs = P(None, "row", None, "col")
    return jax.shard_map(
        per_device, mesh=mesh, in_specs=in_specs, out_specs=out_specs, check_vma=False
    )
```

```python
import functools

import jax
import jax.numpy as jnp
from jax import lax
from jax.experimental import pallas as pl
from jax.experimental.pallas import tpu as pltpu
from jax.sharding import PartitionSpec as P

MESH = pl.DeviceIdType.MESH
VMEM_LIMIT = 48 * 1024 * 1024


def product(left, right, contract):
    return lax.dot_general(
        left,
        right,
        (contract, ((), ())),
        precision=lax.Precision.HIGHEST,
        preferred_element_type=jnp.float32,
    )


TN = ((0,), (0,))
NN = ((1,), (0,))
NT = ((1,), (1,))


def exchange_start(source, slots, send_sem, recv_sem, cols):
    c = lax.axis_index("col")
    r = lax.axis_index("row")
    copies = []
    for step in range(1, cols):
        copy = pltpu.make_async_remote_copy(
            src_ref=source,
            dst_ref=slots.at[step - 1],
            send_sem=send_sem.at[step - 1],
            recv_sem=recv_sem.at[step - 1],
            device_id=(r, lax.rem(c + step, cols)),
            device_id_type=MESH,
        )
        copy.start()
        copies.append(copy)
    return copies


def plane_of(rows, cols):
    plane = cols
    while plane * plane < rows or rows % plane:
        plane += cols
    return plane


def across(source, dest, rows, cols, target_col, send_sem, recv_sem, wait):
    r = lax.axis_index("row")
    plane = plane_of(rows, cols)

    def body(step, carry):
        copy = pltpu.make_async_remote_copy(
            src_ref=source,
            dst_ref=dest.at[r // cols],
            send_sem=send_sem.at[step * plane],
            recv_sem=recv_sem.at[r // cols],
            device_id=(lax.rem(r + step * plane, rows), target_col),
            device_id_type=MESH,
        )
        if wait:
            copy.wait_send()
        else:
            copy.start()
        return carry

    lax.fori_loop(1, rows // plane, body, 0)


def within(source, dest, rows, cols, send_sem, recv_sem, wait):
    r = lax.axis_index("row")
    c = lax.axis_index("col")
    plane = plane_of(rows, cols)
    base = (r // plane) * plane
    place = lax.rem(r, plane)

    def body(step, carry):
        slot = lax.rem(r + step * plane, rows) // cols
        if not wait:

            @pl.when(step > 0)
            def _():
                arrive(source, dest, slot, recv_sem)

        for other in range(1, plane):
            copy = pltpu.make_async_remote_copy(
                src_ref=dest.at[slot],
                dst_ref=dest.at[slot],
                send_sem=send_sem.at[step * plane + other],
                recv_sem=recv_sem.at[slot],
                device_id=(base + lax.rem(place + other, plane), c),
                device_id_type=MESH,
            )
            if wait:
                copy.wait_send()
            else:
                copy.start()
        return carry

    lax.fori_loop(0, rows // plane, body, 0)


def arrive(source, dest, slot, recv_sem):
    pltpu.make_async_remote_copy(
        src_ref=source,
        dst_ref=dest.at[slot],
        send_sem=recv_sem.at[slot],
        recv_sem=recv_sem.at[slot],
        device_id=(lax.axis_index("row"), lax.axis_index("col")),
        device_id_type=MESH,
    ).wait_recv()


BLOCK = 16


def columns_of(block):
    size, lanes = block.shape[0], 128
    return [jnp.broadcast_to(block[:, j : j + 1], (size, lanes)) for j in range(size)]


def small_cholesky_inverse(block):
    size = block.shape[0]
    cols = columns_of(block)
    row = lax.broadcasted_iota(jnp.int32, (size, 128), 0)
    lane = lax.broadcasted_iota(jnp.int32, (size, 128), 1)
    inv = (row == lane).astype(jnp.float32)
    for j in range(size):
        scale = lax.rsqrt(cols[j][j : j + 1])
        factor = cols[j] * scale
        for k in range(j + 1, size):
            cols[k] = cols[k] - factor * factor[k : k + 1]
        pivot = inv[j : j + 1] * scale
        below = jnp.where(row > j, factor, 0.0)
        inv = jnp.where(row == j, pivot, inv - below * pivot)
    return inv[:, :size]


def small_inverse(block):
    size = block.shape[0]
    cols = columns_of(block)
    row = lax.broadcasted_iota(jnp.int32, (size, 128), 0)
    lane = lax.broadcasted_iota(jnp.int32, (size, 128), 1)
    inv = (row == lane).astype(jnp.float32)
    for j in range(size):
        scale = 1.0 / cols[j][j : j + 1]
        others = jnp.where(row == j, 0.0, cols[j])
        for k in range(j + 1, size):
            pivot = cols[k][j : j + 1] * scale
            cols[k] = jnp.where(row == j, pivot, cols[k] - others * pivot)
        pivot = inv[j : j + 1] * scale
        inv = jnp.where(row == j, pivot, inv - others * pivot)
    return inv[:, :size]


def unit(width):
    row = lax.broadcasted_iota(jnp.int32, (width, width), 0)
    lane = lax.broadcasted_iota(jnp.int32, (width, width), 1)
    return (row == lane).astype(jnp.float32)


def cholesky_inverse(gram):
    width = gram.shape[0]
    step = min(BLOCK, width)
    rest = jnp.concatenate([gram, unit(width)], axis=1)
    done = []
    for start in range(0, width, step):
        small = small_cholesky_inverse(rest[:step, start : start + step])
        lead = product(small, rest[:step], NN)
        done.append(lead[:, width:])
        if start + step < width:
            rest = rest[step:] - product(lead[:, start + step : width], lead, TN)
    return jnp.concatenate(done, axis=0)


def full_inverse(matrix):
    width = matrix.shape[0]
    step = min(BLOCK, width)
    work = jnp.concatenate([matrix, unit(width)], axis=1)
    row = lax.broadcasted_iota(jnp.int32, (width, step), 0)
    for start in range(0, width, step):
        stop = start + step
        small = small_inverse(work[start:stop, start:stop])
        lead = product(small, work[start:stop], NN)
        inside = jnp.logical_and(row >= start, row < stop)
        work = work - product(jnp.where(inside, 0.0, work[:, start:stop]), lead, NN)
        pieces = [work[:start], lead, work[stop:]]
        work = jnp.concatenate([piece for piece in pieces if piece.shape[0]], axis=0)
    return work[:, width:]


def greet(rows, cols):
    r = lax.axis_index("row")
    c = lax.axis_index("col")
    barrier = pltpu.get_barrier_semaphore()
    plane = plane_of(rows, cols)
    base = (r // plane) * plane
    place = lax.rem(r, plane)

    @pl.when(lax.rem(r, cols) == c)
    def _():
        for step in range(1, rows // plane):
            root = lax.rem(r + step * plane, rows)
            pl.semaphore_signal(barrier, inc=1, device_id=(root, 0), device_id_type=MESH)

            @pl.when(c != 0)
            def _():
                pl.semaphore_signal(barrier, inc=1, device_id=(root, c), device_id_type=MESH)

    for index in range(plane // cols):
        other = index * cols + c

        @pl.when(other != place)
        def _():
            pl.semaphore_signal(barrier, inc=1, device_id=(base + other, c), device_id_type=MESH)

    for step in range(1, cols):
        pl.semaphore_signal(
            barrier, inc=1, device_id=(r, lax.rem(c + step, cols)), device_id_type=MESH
        )


def greeted(rows, cols, is_root, sends):
    barrier = pltpu.get_barrier_semaphore()
    plane = plane_of(rows, cols)
    outer = rows // plane - 1

    @pl.when(sends)
    def _():
        pl.semaphore_wait(barrier, outer + plane - 1 + cols - 1)

    @pl.when(jnp.logical_and(is_root, jnp.logical_not(sends)))
    def _():
        pl.semaphore_wait(barrier, outer + cols - 1)

    @pl.when(jnp.logical_not(jnp.logical_or(is_root, sends)))
    def _():
        pl.semaphore_wait(barrier, cols - 1)


def split(value):
    high = value.astype(jnp.bfloat16)
    return high, (value - high.astype(jnp.float32)).astype(jnp.bfloat16)


def product3(left, right, contract):
    def one(a, b):
        return lax.dot_general(a, b, (contract, ((), ())), preferred_element_type=jnp.float32)

    return one(left[0], right[0]) + (one(left[0], right[1]) + one(left[1], right[0]))


def panel_kernel(
    rows, cols, local_ref, change_ref,
    tiles, own, parts, slots, vecs, image, own_image, part_slots, mid, mid_slots, wide_high, wide_low,
    send_sem, recv_sem, own_send, own_recv, ex_send, ex_recv,
    im_send, im_recv, part_send, part_recv, mid_send, mid_recv,
):
    r = lax.axis_index("row")
    c = lax.axis_index("col")
    width = own.shape[0]
    is_root = c == 0
    count = rows // cols
    slot_own = r // cols
    own_col = lax.rem(r, cols)
    sends = own_col == c
    plane = plane_of(rows, cols)
    place = lax.rem(r, plane)
    identity = unit(width)
    greet(rows, cols)

    @pl.when(is_root)
    def _():
        own[...] = local_ref[0, :, 0, :]

    greeted(rows, cols, is_root, sends)

    @pl.when(is_root)
    def _():
        for peer in range(1, cols):
            pltpu.make_async_remote_copy(
                src_ref=own, dst_ref=own, send_sem=own_send.at[peer - 1],
                recv_sem=own_recv, device_id=(r, peer), device_id_type=MESH,
            ).start()
        across(own, tiles, rows, cols, own_col, send_sem, recv_sem, False)

    for slot in range(count):
        columns = slice(slot * width, slot * width + width)
        wide_high[:, columns], wide_low[:, columns] = split(local_ref[0, :, slot, :])

    @pl.when(jnp.logical_not(is_root))
    def _():
        pltpu.make_async_remote_copy(
            src_ref=own, dst_ref=own, send_sem=own_recv,
            recv_sem=own_recv, device_id=(r, c), device_id_type=MESH,
        ).wait_recv()

    @pl.when(sends)
    def _():
        tiles[slot_own] = own[...]
        within(own, tiles, rows, cols, send_sem, recv_sem, False)

    def arrive_rest(source, dest, sem):
        def body(slot, carry):
            away = lax.rem(slot * cols + c, plane) != place

            @pl.when(jnp.logical_or(away, jnp.logical_not(sends)))
            def _():
                arrive(source, dest, slot, sem)

            return carry

        lax.fori_loop(0, count, body, 0)

    arrive_rest(own, tiles, recv_sem)
    flat = tiles[...].reshape(count * width, width)
    place_row = lax.broadcasted_iota(jnp.int32, flat.shape, 0)
    flat = jnp.where(jnp.logical_and(place_row < width, c == 0), 0.0, flat)
    parts[0] = product(flat, flat, TN)
    parts[1] = jnp.where(c == 1 % cols, tiles[1 // cols], 0.0)
    for copy in exchange_start(parts, slots, ex_send, ex_recv, cols):
        copy.wait()
    sums = parts[...]
    for step in range(cols - 1):
        sums = sums + slots[step]
    inverse = cholesky_inverse(sums[0])

    def vectors(tile, block):
        keep = (tile != 0).astype(jnp.float32)
        first = (tile == 1).astype(jnp.float32)
        return product(block, inverse, NT) * keep + identity * first

    vecs[...] = product(flat, inverse, NT).reshape(vecs.shape)
    vecs[1 // cols] += identity * (c == 1 % cols).astype(jnp.float32)
    flat_vec = vecs[...].reshape(count * width, width)
    vec_parts = split(flat_vec)
    mid[...] = product3((wide_high[...], wide_low[...]), vec_parts, NN)
    copies = exchange_start(mid, part_slots, part_send, part_recv, cols)
    row_vec = vectors(r, own[...])
    for copy in copies:
        copy.wait()
    total = mid[...]
    for step in range(cols - 1):
        total = total + part_slots[step]
    own_image[...] = total

    @pl.when(sends)
    def _():
        across(own_image, image, rows, cols, c, im_send, im_recv, False)
        image[slot_own] = total
        within(own_image, image, rows, cols, im_send, im_recv, False)

    coupling = full_inverse(identity + product(inverse, sums[1], NT))
    upd_rows = product(total, coupling, NN)

    arrive_rest(own_image, image, im_recv)
    flat_image = split(image[...].reshape(count * width, width))
    mid[...] = product3(vec_parts, flat_image, TN)
    copies = exchange_start(mid, mid_slots, mid_send, mid_recv, cols)
    upd_cols = product3(flat_image, split(coupling), NN)
    for copy in copies:
        copy.wait()
    middle = mid[...]
    for step in range(cols - 1):
        middle = middle + mid_slots[step]
    half = 0.5 * product(coupling, product(middle, coupling, NN), TN)
    upd_rows = upd_rows - product(row_vec, half, NN)
    upd_cols = upd_cols - product3(vec_parts, split(half), NN)
    left = split(jnp.concatenate([upd_rows, row_vec], axis=1))
    right = split(jnp.concatenate([flat_vec, upd_cols], axis=1))
    change_ref[...] = product3(left, right, NT)

    @pl.when(is_root)
    def _():
        for peer in range(1, cols):
            pltpu.make_async_remote_copy(
                src_ref=own, dst_ref=own, send_sem=own_send.at[peer - 1],
                recv_sem=own_recv, device_id=(r, peer), device_id_type=MESH,
            ).wait_send()
        across(own, tiles, rows, cols, own_col, send_sem, recv_sem, True)

    @pl.when(sends)
    def _():
        within(own, tiles, rows, cols, send_sem, recv_sem, True)
        across(own_image, image, rows, cols, c, im_send, im_recv, True)
        within(own_image, image, rows, cols, im_send, im_recv, True)


def per_device(matrix):
    _, width, count, _ = matrix.shape
    rows = lax.axis_size("row")
    cols = lax.axis_size("col")
    dma = pltpu.SemaphoreType.DMA

    def buffer(*shape):
        return pltpu.VMEM((*shape, width, width), jnp.float32)

    change = pl.pallas_call(
        functools.partial(panel_kernel, rows, cols),
        out_shape=jax.ShapeDtypeStruct((width, count * width), jnp.float32),
        in_specs=[pl.BlockSpec(memory_space=pltpu.VMEM)],
        out_specs=pl.BlockSpec(memory_space=pltpu.VMEM),
        scratch_shapes=[
            buffer(count), buffer(), buffer(2), buffer(cols - 1, 2), buffer(count), buffer(count),
            buffer(), buffer(cols - 1), buffer(), buffer(cols - 1),
            pltpu.VMEM((width, count * width), jnp.bfloat16),
            pltpu.VMEM((width, count * width), jnp.bfloat16),
            dma((rows,)), dma((count,)), dma((cols - 1,)), dma, dma((cols - 1,)), dma((cols - 1,)),
            dma((rows,)), dma((count,)), dma((cols - 1,)), dma((cols - 1,)),
            dma((cols - 1,)), dma((cols - 1,)),
        ],
        compiler_params=pltpu.CompilerParams(
            collective_id=0, has_side_effects=True, vmem_limit_bytes=VMEM_LIMIT
        ),
    )(matrix)
    return matrix - change.reshape(matrix.shape)


def solution(mesh):
    in_specs = (P(None, "row", None, "col"),)
    out_specs = P(None, "row", None, "col")
    return jax.shard_map(
        per_device, mesh=mesh, in_specs=in_specs, out_specs=out_specs, check_vma=False
    )
```

```python
import functools

import jax
import jax.numpy as jnp
from jax import lax
from jax.experimental import pallas as pl
from jax.experimental.pallas import tpu as pltpu
from jax.sharding import PartitionSpec as P

MESH = pl.DeviceIdType.MESH
VMEM_LIMIT = 48 * 1024 * 1024


def product(left, right, contract):
    return lax.dot_general(
        left,
        right,
        (contract, ((), ())),
        precision=lax.Precision.HIGHEST,
        preferred_element_type=jnp.float32,
    )


TN = ((0,), (0,))
NN = ((1,), (0,))
NT = ((1,), (1,))


def exchange_start(source, slots, send_sem, recv_sem, cols):
    c = lax.axis_index("col")
    r = lax.axis_index("row")
    copies = []
    for step in range(1, cols):
        copy = pltpu.make_async_remote_copy(
            src_ref=source,
            dst_ref=slots.at[step - 1],
            send_sem=send_sem.at[step - 1],
            recv_sem=recv_sem.at[step - 1],
            device_id=(r, lax.rem(c + step, cols)),
            device_id_type=MESH,
        )
        copy.start()
        copies.append(copy)
    return copies


def plane_of(rows, cols):
    plane = cols
    while plane * plane < rows or rows % plane:
        plane += cols
    return plane


def across(source, dest, rows, cols, target_col, send_sem, recv_sem, wait):
    r = lax.axis_index("row")
    plane = plane_of(rows, cols)

    def body(step, carry):
        copy = pltpu.make_async_remote_copy(
            src_ref=source,
            dst_ref=dest.at[r // cols],
            send_sem=send_sem.at[step * plane],
            recv_sem=recv_sem.at[r // cols],
            device_id=(lax.rem(r + step * plane, rows), target_col),
            device_id_type=MESH,
        )
        if wait:
            copy.wait_send()
        else:
            copy.start()
        return carry

    lax.fori_loop(1, rows // plane, body, 0)


def within(source, dest, rows, cols, send_sem, recv_sem, wait):
    r = lax.axis_index("row")
    c = lax.axis_index("col")
    plane = plane_of(rows, cols)
    base = (r // plane) * plane
    place = lax.rem(r, plane)

    def body(step, carry):
        slot = lax.rem(r + step * plane, rows) // cols
        if not wait:

            @pl.when(step > 0)
            def _():
                arrive(source, dest, slot, recv_sem)

        for other in range(1, plane):
            copy = pltpu.make_async_remote_copy(
                src_ref=dest.at[slot],
                dst_ref=dest.at[slot],
                send_sem=send_sem.at[step * plane + other],
                recv_sem=recv_sem.at[slot],
                device_id=(base + lax.rem(place + other, plane), c),
                device_id_type=MESH,
            )
            if wait:
                copy.wait_send()
            else:
                copy.start()
        return carry

    lax.fori_loop(0, rows // plane, body, 0)


def arrive(source, dest, slot, recv_sem):
    pltpu.make_async_remote_copy(
        src_ref=source,
        dst_ref=dest.at[slot],
        send_sem=recv_sem.at[slot],
        recv_sem=recv_sem.at[slot],
        device_id=(lax.axis_index("row"), lax.axis_index("col")),
        device_id_type=MESH,
    ).wait_recv()


BLOCK = 32


def columns_of(block):
    size, lanes = block.shape[0], 128
    return [jnp.broadcast_to(block[:, j : j + 1], (size, lanes)) for j in range(size)]


def small_cholesky_inverse(block):
    size = block.shape[0]
    cols = columns_of(block)
    row = lax.broadcasted_iota(jnp.int32, (size, 128), 0)
    lane = lax.broadcasted_iota(jnp.int32, (size, 128), 1)
    inv = (row == lane).astype(jnp.float32)
    for j in range(size):
        scale = lax.rsqrt(cols[j][j : j + 1])
        factor = cols[j] * scale
        for k in range(j + 1, size):
            cols[k] = cols[k] - factor * factor[k : k + 1]
        pivot = inv[j : j + 1] * scale
        below = jnp.where(row > j, factor, 0.0)
        inv = jnp.where(row == j, pivot, inv - below * pivot)
    return inv[:, :size]


def small_inverse(block):
    size = block.shape[0]
    cols = columns_of(block)
    row = lax.broadcasted_iota(jnp.int32, (size, 128), 0)
    lane = lax.broadcasted_iota(jnp.int32, (size, 128), 1)
    inv = (row == lane).astype(jnp.float32)
    for j in range(size):
        scale = 1.0 / cols[j][j : j + 1]
        others = jnp.where(row == j, 0.0, cols[j])
        for k in range(j + 1, size):
            pivot = cols[k][j : j + 1] * scale
            cols[k] = jnp.where(row == j, pivot, cols[k] - others * pivot)
        pivot = inv[j : j + 1] * scale
        inv = jnp.where(row == j, pivot, inv - others * pivot)
    return inv[:, :size]


def unit(width):
    row = lax.broadcasted_iota(jnp.int32, (width, width), 0)
    lane = lax.broadcasted_iota(jnp.int32, (width, width), 1)
    return (row == lane).astype(jnp.float32)


def cholesky_inverse(gram):
    width = gram.shape[0]
    step = min(BLOCK, width)
    rest = jnp.concatenate([gram, unit(width)], axis=1)
    done = []
    for start in range(0, width, step):
        small = small_cholesky_inverse(rest[:step, start : start + step])
        lead = product(small, rest[:step], NN)
        done.append(lead[:, width:])
        if start + step < width:
            rest = rest[step:] - product(lead[:, start + step : width], lead, TN)
    return jnp.concatenate(done, axis=0)


def full_inverse(matrix):
    width = matrix.shape[0]
    step = min(BLOCK, width)
    work = jnp.concatenate([matrix, unit(width)], axis=1)
    row = lax.broadcasted_iota(jnp.int32, (width, step), 0)
    for start in range(0, width, step):
        stop = start + step
        small = small_inverse(work[start:stop, start:stop])
        lead = product(small, work[start:stop], NN)
        inside = jnp.logical_and(row >= start, row < stop)
        work = work - product(jnp.where(inside, 0.0, work[:, start:stop]), lead, NN)
        pieces = [work[:start], lead, work[stop:]]
        work = jnp.concatenate([piece for piece in pieces if piece.shape[0]], axis=0)
    return work[:, width:]


def greet(rows, cols):
    r = lax.axis_index("row")
    c = lax.axis_index("col")
    barrier = pltpu.get_barrier_semaphore()
    plane = plane_of(rows, cols)
    base = (r // plane) * plane
    place = lax.rem(r, plane)

    @pl.when(lax.rem(r, cols) == c)
    def _():
        for step in range(1, rows // plane):
            root = lax.rem(r + step * plane, rows)
            pl.semaphore_signal(barrier, inc=1, device_id=(root, 0), device_id_type=MESH)

            @pl.when(c != 0)
            def _():
                pl.semaphore_signal(barrier, inc=1, device_id=(root, c), device_id_type=MESH)

    for index in range(plane // cols):
        other = index * cols + c

        @pl.when(other != place)
        def _():
            pl.semaphore_signal(barrier, inc=1, device_id=(base + other, c), device_id_type=MESH)

    for step in range(1, cols):
        pl.semaphore_signal(
            barrier, inc=1, device_id=(r, lax.rem(c + step, cols)), device_id_type=MESH
        )


def greeted(rows, cols, is_root, sends):
    barrier = pltpu.get_barrier_semaphore()
    plane = plane_of(rows, cols)
    outer = rows // plane - 1

    @pl.when(sends)
    def _():
        pl.semaphore_wait(barrier, outer + plane - 1 + cols - 1)

    @pl.when(jnp.logical_and(is_root, jnp.logical_not(sends)))
    def _():
        pl.semaphore_wait(barrier, outer + cols - 1)

    @pl.when(jnp.logical_not(jnp.logical_or(is_root, sends)))
    def _():
        pl.semaphore_wait(barrier, cols - 1)


def split(value):
    high = value.astype(jnp.bfloat16)
    return high, (value - high.astype(jnp.float32)).astype(jnp.bfloat16)


def product3(left, right, contract):
    def one(a, b):
        return lax.dot_general(a, b, (contract, ((), ())), preferred_element_type=jnp.float32)

    return one(left[0], right[0]) + (one(left[0], right[1]) + one(left[1], right[0]))


def panel_kernel(
    rows, cols, local_ref, change_ref,
    tiles, own, parts, slots, vecs, image, own_image, part_slots, mid, mid_slots, wide_high, wide_low,
    send_sem, recv_sem, own_send, own_recv, ex_send, ex_recv,
    im_send, im_recv, part_send, part_recv, mid_send, mid_recv,
):
    r = lax.axis_index("row")
    c = lax.axis_index("col")
    width = own.shape[0]
    is_root = c == 0
    count = rows // cols
    slot_own = r // cols
    own_col = lax.rem(r, cols)
    sends = own_col == c
    plane = plane_of(rows, cols)
    place = lax.rem(r, plane)
    identity = unit(width)
    greet(rows, cols)

    @pl.when(is_root)
    def _():
        own[...] = local_ref[0, :, 0, :]

    greeted(rows, cols, is_root, sends)

    @pl.when(is_root)
    def _():
        for peer in range(1, cols):
            pltpu.make_async_remote_copy(
                src_ref=own, dst_ref=own, send_sem=own_send.at[peer - 1],
                recv_sem=own_recv, device_id=(r, peer), device_id_type=MESH,
            ).start()
        across(own, tiles, rows, cols, own_col, send_sem, recv_sem, False)

    for slot in range(count):
        columns = slice(slot * width, slot * width + width)
        wide_high[:, columns], wide_low[:, columns] = split(local_ref[0, :, slot, :])

    @pl.when(jnp.logical_not(is_root))
    def _():
        pltpu.make_async_remote_copy(
            src_ref=own, dst_ref=own, send_sem=own_recv,
            recv_sem=own_recv, device_id=(r, c), device_id_type=MESH,
        ).wait_recv()

    @pl.when(sends)
    def _():
        tiles[slot_own] = own[...]
        within(own, tiles, rows, cols, send_sem, recv_sem, False)

    def arrive_rest(source, dest, sem):
        def body(slot, carry):
            away = lax.rem(slot * cols + c, plane) != place

            @pl.when(jnp.logical_or(away, jnp.logical_not(sends)))
            def _():
                arrive(source, dest, slot, sem)

            return carry

        lax.fori_loop(0, count, body, 0)

    arrive_rest(own, tiles, recv_sem)
    flat = tiles[...].reshape(count * width, width)
    place_row = lax.broadcasted_iota(jnp.int32, flat.shape, 0)
    flat = jnp.where(jnp.logical_and(place_row < width, c == 0), 0.0, flat)
    parts[0] = product(flat, flat, TN)
    parts[1] = jnp.where(c == 1 % cols, tiles[1 // cols], 0.0)
    for copy in exchange_start(parts, slots, ex_send, ex_recv, cols):
        copy.wait()
    sums = parts[...]
    for step in range(cols - 1):
        sums = sums + slots[step]
    inverse = cholesky_inverse(sums[0])

    def vectors(tile, block):
        keep = (tile != 0).astype(jnp.float32)
        first = (tile == 1).astype(jnp.float32)
        return product(block, inverse, NT) * keep + identity * first

    vecs[...] = product(flat, inverse, NT).reshape(vecs.shape)
    vecs[1 // cols] += identity * (c == 1 % cols).astype(jnp.float32)
    flat_vec = vecs[...].reshape(count * width, width)
    vec_parts = split(flat_vec)
    mid[...] = product3((wide_high[...], wide_low[...]), vec_parts, NN)
    copies = exchange_start(mid, part_slots, part_send, part_recv, cols)
    row_vec = vectors(r, own[...])
    for copy in copies:
        copy.wait()
    total = mid[...]
    for step in range(cols - 1):
        total = total + part_slots[step]
    own_image[...] = total

    @pl.when(sends)
    def _():
        across(own_image, image, rows, cols, c, im_send, im_recv, False)
        image[slot_own] = total
        within(own_image, image, rows, cols, im_send, im_recv, False)

    coupling = full_inverse(identity + product(inverse, sums[1], NT))
    upd_rows = product(total, coupling, NN)

    arrive_rest(own_image, image, im_recv)
    flat_image = split(image[...].reshape(count * width, width))
    mid[...] = product3(vec_parts, flat_image, TN)
    copies = exchange_start(mid, mid_slots, mid_send, mid_recv, cols)
    upd_cols = product3(flat_image, split(coupling), NN)
    for copy in copies:
        copy.wait()
    middle = mid[...]
    for step in range(cols - 1):
        middle = middle + mid_slots[step]
    half = 0.5 * product(coupling, product(middle, coupling, NN), TN)
    upd_rows = upd_rows - product(row_vec, half, NN)
    upd_cols = upd_cols - product3(vec_parts, split(half), NN)
    left = split(jnp.concatenate([upd_rows, row_vec], axis=1))
    right = split(jnp.concatenate([flat_vec, upd_cols], axis=1))
    change_ref[...] = product3(left, right, NT)

    @pl.when(is_root)
    def _():
        for peer in range(1, cols):
            pltpu.make_async_remote_copy(
                src_ref=own, dst_ref=own, send_sem=own_send.at[peer - 1],
                recv_sem=own_recv, device_id=(r, peer), device_id_type=MESH,
            ).wait_send()
        across(own, tiles, rows, cols, own_col, send_sem, recv_sem, True)

    @pl.when(sends)
    def _():
        within(own, tiles, rows, cols, send_sem, recv_sem, True)
        across(own_image, image, rows, cols, c, im_send, im_recv, True)
        within(own_image, image, rows, cols, im_send, im_recv, True)


def per_device(matrix):
    _, width, count, _ = matrix.shape
    rows = lax.axis_size("row")
    cols = lax.axis_size("col")
    dma = pltpu.SemaphoreType.DMA

    def buffer(*shape):
        return pltpu.VMEM((*shape, width, width), jnp.float32)

    change = pl.pallas_call(
        functools.partial(panel_kernel, rows, cols),
        out_shape=jax.ShapeDtypeStruct((width, count * width), jnp.float32),
        in_specs=[pl.BlockSpec(memory_space=pltpu.VMEM)],
        out_specs=pl.BlockSpec(memory_space=pltpu.VMEM),
        scratch_shapes=[
            buffer(count), buffer(), buffer(2), buffer(cols - 1, 2), buffer(count), buffer(count),
            buffer(), buffer(cols - 1), buffer(), buffer(cols - 1),
            pltpu.VMEM((width, count * width), jnp.bfloat16),
            pltpu.VMEM((width, count * width), jnp.bfloat16),
            dma((rows,)), dma((count,)), dma((cols - 1,)), dma, dma((cols - 1,)), dma((cols - 1,)),
            dma((rows,)), dma((count,)), dma((cols - 1,)), dma((cols - 1,)),
            dma((cols - 1,)), dma((cols - 1,)),
        ],
        compiler_params=pltpu.CompilerParams(
            collective_id=0, has_side_effects=True, vmem_limit_bytes=VMEM_LIMIT
        ),
    )(matrix)
    return matrix - change.reshape(matrix.shape)


def solution(mesh):
    in_specs = (P(None, "row", None, "col"),)
    out_specs = P(None, "row", None, "col")
    return jax.shard_map(
        per_device, mesh=mesh, in_specs=in_specs, out_specs=out_specs, check_vma=False
    )
```
